32 devices in a mesh: groups: 2 (over y), tensor: 4 (over z), dp: 4 (over x, core).
Axes of the slice: x: 2, y: 2, z: 4, core: 2. Of those that a mesh axis runs over, the one named last changes fastest.
Arguments:
- out_grad: bfloat16 [4, 1280, 4096], P('dp', ('groups', 'tensor')), parts along dimension 1, may hold values from -6 to 6
- gate_pre: bfloat16 [4, 1280, 14336], P('dp', 'groups', 'tensor'), parts along dimension 1, may hold values from -8 to 8
- up_pre: bfloat16 [4, 1280, 14336], P('dp', 'groups', 'tensor'), parts along dimension 1, may hold values from -6 to 6
- down_weight: bfloat16 [14336, 4096], P('tensor'), may hold values from -0.046875 to 0.046875
Outputs:
- gate_grad: bfloat16 [4, 1280, 14336], P('dp', 'groups', 'tensor'), parts along dimension 1
- up_grad: bfloat16 [4, 1280, 14336], P('dp', 'groups', 'tensor'), parts along dimension 1
- down_grad: bfloat16 [28672, 4096], P(('groups', 'tensor'), 'dp'), parts along dimension 0
The draws below stay inside these ranges and needn't reach their ends.
There are 2 independent parts, one for each index of `groups`. The reference program is written for one: setup_inputs(seed, part) draws one part's arguments, and reference() takes and returns one part's arrays. A program takes and returns all parts, laid end to end along the dimension named above; an argument that names none is the same for every part. Nothing has to cross between parts.
All inputs are finite; a program needn't handle non-finite values.
Results may differ from the reference program's by a relative error of at most 0.014.
Values may be sent and summed in bfloat16 or wider, within the bound.
No kernel may reach another device: no remote copies, remote signals or barrier semaphores. Data moves between devices by JAX's collectives and lax.ppermute only.
A program may use at most 128 MiB of HBM per device.

```python
import math
import jax
import jax.numpy as jnp
from jax import lax

D = 4096
FF = 14336
TOK_GROUP = 640
DATA = 4
TOKENS = 2560


def block_scale(rng, extent, pieces, low, high):
    gain, own = 1.0, jax.random.fold_in(rng, 6)
    for position, parts in pieces:
        draws = jnp.exp(jax.random.uniform(jax.random.fold_in(own, position), (parts,), jnp.float32, low / len(pieces), high / len(pieces)))
        gain = gain * jnp.repeat(draws, extent[position] // parts).reshape([-1 if axis == position else 1 for axis in range(len(extent))])
    return gain


def centred(rng, extent, width, reach, pieces=(), kind=jnp.bfloat16):
    level = block_scale(rng, extent, pieces, -0.22, 0.18) if pieces else 1.0
    drawn = jax.random.normal(rng, extent, jnp.float32) * width * level
    return jnp.minimum(jnp.maximum(drawn, -reach), reach).astype(kind)


def setup_inputs(seed: int = 0, part: int = 0) -> dict:
    arg_keys = jax.random.split(jax.random.key(seed), 5)
    own_keys = jax.random.split(jax.random.fold_in(arg_keys[4], part), 5)
    return {
        "out_grad": centred(own_keys[0], (DATA, TOK_GROUP, D), 1.0, 6.0, ((0, 4), (1, 4))),
        "gate_pre": centred(own_keys[1], (DATA, TOK_GROUP, FF), 1.5, 8.0, ((0, 4), (2, 4))),
        "up_pre": centred(own_keys[2], (DATA, TOK_GROUP, FF), 1.0, 6.0, ((0, 4), (2, 4))),
        "down_weight": centred(arg_keys[3], (FF, D), FF ** -0.5, 0.046875, ((0, 4),)),
    }


def reference(out_grad, gate_pre, up_pre, down_weight):
    gate = gate_pre.astype(jnp.float32)
    up = up_pre.astype(jnp.float32)
    sig = jax.nn.sigmoid(gate)
    act = gate * sig
    hidden = (act * up).astype(jnp.bfloat16)
    scale = 1.0 / math.sqrt(TOKENS)
    indices = jnp.arange(DATA)

    def group_term(total, index):
        term = jnp.dot(hidden[index].T, out_grad[index], preferred_element_type=jnp.float32) * scale
        rounded = lax.optimization_barrier(term.astype(jnp.bfloat16))
        return (total + rounded.astype(jnp.float32), None)
    total, _ = lax.scan(group_term, jnp.zeros((FF, D), jnp.float32), indices)

    def group_grad(index):
        return jnp.dot(out_grad[index], down_weight.T, preferred_element_type=jnp.float32)
    hidden_grad = lax.map(group_grad, indices)
    gate_grad = (hidden_grad * up * sig * (1.0 + gate * (1.0 - sig))).astype(jnp.bfloat16)
    up_grad = (hidden_grad * act).astype(jnp.bfloat16)
    return (gate_grad, up_grad, total.astype(jnp.bfloat16))
```

```python
import functools
import math

import jax
import jax.numpy as jnp
from jax import lax
from jax.experimental import pallas as pl
from jax.experimental.pallas import tpu as pltpu
from jax.sharding import PartitionSpec as P

VMEM_LIMIT = 16 * 1024 * 1024
F32, BF16 = jnp.float32, jnp.bfloat16
ANY_SPEC = pl.BlockSpec(memory_space=pl.ANY)
VMEM_SPEC = pl.BlockSpec(memory_space=pltpu.VMEM)


def pick_tile(extent, cap):
    return max(t for t in range(128, cap + 1, 128) if extent % t == 0)


def together(*values):
    return lax.optimization_barrier(values)


def sigmoid(x):
    return 0.5 + 0.5 * jnp.tanh(0.5 * x)


def contract_last(a, b):
    return lax.dot_general(a, b, (((1,), (1,)), ((), ())), preferred_element_type=F32)


def contract_first(a, b):
    return lax.dot_general(a, b, (((0,), (0,)), ((), ())), preferred_element_type=F32)


def in_vmem(value):
    return pltpu.with_memory_space_constraint(value, pltpu.VMEM)


def in_hbm(values):
    return [pltpu.with_memory_space_constraint(v, pltpu.HBM) for v in values]


def place_shards(parts, half, into, sem, start):
    act = (lambda c: c.start()) if start else (lambda c: c.wait())
    z = lax.axis_index("tensor")
    rows = parts[0].shape[0]

    def place(ref, shard, slot):
        at = shard if half == "all" else shard % 2
        at = pl.multiple_of(at * rows, rows)
        act(pltpu.make_async_copy(ref, into.at[pl.ds(at, rows)], sem.at[slot]))

    if half != "late":
        place(parts[0], z, 0)
        place(parts[1], z + 1 - 2 * (z % 2), 1)
    if half != "early":
        b0, b1, c0, c1 = parts[-4:]
        first, second = jnp.where(z < 2, 2, 1), jnp.where(z < 2, 3, 0)
        middle = jnp.logical_or(z == 1, z == 2)

        @pl.when(middle)
        def _():
            place(b0, first, 2)
            place(b1, second, 3)

        @pl.when(jnp.logical_not(middle))
        def _():
            place(c0, first, 2)
            place(c1, second, 3)


def move_kernel(n_parts, *refs):
    parts, (into, sem) = refs[:n_parts], refs[-2:]
    first = refs[n_parts : -2]
    rows = 4 * parts[0].shape[0]
    if first:
        copy = pltpu.make_async_copy(first[0], into.at[pl.ds(0, rows)], sem.at[4])
        copy.start()
        into = into.at[pl.ds(rows, rows)]
    for start in (True, False):
        place_shards(parts, "all", into, sem, start)
    if first:
        copy.wait()


def in_token_order(parts, first=()):
    rows, cols = parts[0].shape
    return pl.pallas_call(
        functools.partial(move_kernel, len(parts)),
        in_specs=[ANY_SPEC] * len(parts) + [VMEM_SPEC] * len(first),
        out_specs=VMEM_SPEC,
        out_shape=pltpu.VMEM((rows * 4 * (1 + len(first)), cols), BF16),
        scratch_shapes=[pltpu.SemaphoreType.DMA((5,))],
        compiler_params=pltpu.CompilerParams(vmem_limit_bytes=VMEM_LIMIT),
        name="in_token_order",
    )(*parts, *[in_vmem(f) for f in first])


def load_weight_kernel(weight, *refs):
    outs, mark, sem = refs[:-2], refs[-2], refs[-1]
    chip = lax.axis_index("dp") // 2
    copies = []
    for s, out in enumerate(outs):
        width = out.shape[1]
        at = pl.multiple_of(lax.rem(chip + s, len(outs)) * width, width)
        copies.append(pltpu.make_async_copy(weight.at[:, pl.ds(at, width)], out, sem.at[s]))
    for copy in copies:
        copy.start()
    mark[...] = jnp.zeros(mark.shape, mark.dtype)
    for copy in copies:
        copy.wait()


def load_weight(weight, blocks):
    ff, d = weight.shape
    return pl.pallas_call(
        load_weight_kernel,
        in_specs=[ANY_SPEC],
        out_specs=[VMEM_SPEC] * (blocks + 1),
        out_shape=[pltpu.VMEM((ff, d // blocks), BF16)] * blocks + [jax.ShapeDtypeStruct((8, 128), F32)],
        scratch_shapes=[pltpu.SemaphoreType.DMA((blocks,))],
        cost_estimate=pl.CostEstimate(flops=0, bytes_accessed=4 * ff * d, transcendentals=0),
        compiler_params=pltpu.CompilerParams(vmem_limit_bytes=VMEM_LIMIT),
        name="load_weight",
    )(*in_hbm([weight]))


def hidden_kernel(gate_ref, up_ref, hidden_ref):
    gate, up = gate_ref[...].astype(F32), up_ref[...].astype(F32)
    hidden_ref[...] = (gate * sigmoid(gate) * up).astype(BF16)


def factors_kernel(start, gate_ref, up_ref, hidden_ref, gate_by_ref, up_by_ref):
    gate, up = gate_ref[...].astype(F32), up_ref[...].astype(F32)
    sig = sigmoid(gate)
    act = gate * sig
    gate_by_ref[...] = (up * sig * (1.0 + gate * (1.0 - sig))).astype(BF16)
    up_by_ref[...] = act.astype(BF16)
    hidden_ref[...] = (act[:, start:] * up[:, start:]).astype(BF16)


def factors(kernel, gate, up, columns, widths):
    tok = gate.shape[0]
    rows = next(r for r in (64, 32, 16) if tok % r == 0)
    spec = lambda w: pl.BlockSpec((rows, w), lambda i: (i, 0))
    return pl.pallas_call(
        kernel,
        grid=(tok // rows,),
        in_specs=[spec(columns)] * 2,
        out_specs=[spec(w) for w in widths],
        out_shape=[pltpu.HBM((tok, w), BF16) for w in widths],
        cost_estimate=pl.CostEstimate(
            flops=20 * tok * columns, bytes_accessed=2 * tok * (2 * columns + sum(widths)), transcendentals=tok * columns
        ),
        compiler_params=pltpu.CompilerParams(vmem_limit_bytes=VMEM_LIMIT),
        name="factors",
    )(*in_hbm([gate, up]))


def hidden_grad_kernel(half, counts, tile, has_partial, finish, *refs):
    refs = list(refs)
    streams = [[refs.pop(0) for _ in range(count)] for count in counts]
    weights = [refs.pop(0) for _ in counts]
    partial = refs.pop(0) if has_partial else None
    if half == "all":
        lhs = [stream[0] for stream in streams]
    else:
        sem = refs.pop()
        lhs = refs[-len(counts) :]
        refs = refs[: -len(counts)]

        @pl.when(pl.program_id(0) == 0)
        def _():
            for start in (True, False):
                for s, parts in enumerate(streams):
                    place_shards(parts, half, lhs[s], sem.at[s], start)

    at = pl.multiple_of(pl.program_id(0) * tile, tile)
    total = partial[...] if has_partial else None
    for left, weight in zip(lhs, weights):
        term = contract_last(left[...], weight[pl.ds(at, tile), :])
        total = term if total is None else total + term
    if not finish:
        refs[-1][...] = total
        return
    gate_out, up_out = refs[-2:]
    gate_out[...] = (total * refs[0][...].astype(F32)).astype(BF16)
    up_out[...] = (total * refs[1][...].astype(F32)).astype(BF16)


def hidden_grad(half, streams, weights, tok, partial=None, by=None, outs=None):
    ff = weights[0].shape[0]
    rows = tok if half == "all" else tok // 2
    tile = pick_tile(ff, 896)

    def place(i):
        pair = lax.axis_index("tensor") // 2
        return ({"all": 0, "early": pair, "late": 1 - pair}[half], i)

    block = pl.BlockSpec((rows, tile), place)
    part_block = pl.BlockSpec((rows, tile), lambda i: (0, i))
    if half == "all":
        in_specs, args, scratch = [VMEM_SPEC] * len(streams), [in_vmem(s[0]) for s in streams], []
    else:
        args = [part for s in streams for part in s]
        in_specs = [ANY_SPEC] * len(args)
        scratch = [pltpu.VMEM((rows, w.shape[1]), BF16) for w in weights] + [
            pltpu.SemaphoreType.DMA((len(weights), 4))
        ]
    in_specs += [VMEM_SPEC] * len(weights)
    args += [in_vmem(w) for w in weights]
    aliases = {}
    if partial is not None:
        in_specs.append(part_block)
        args += in_hbm([partial])
    if by is not None:
        in_specs += [block] * 2
        args += in_hbm(by)
        out_shape, out_specs = [pltpu.HBM((tok, ff), BF16)] * 2, [block] * 2
        if outs is not None:
            aliases = {len(args): 0, len(args) + 1: 1}
            in_specs += [ANY_SPEC] * 2
            args += in_hbm(outs)
    else:
        out_shape, out_specs = pltpu.HBM((rows, ff), F32), part_block
    return pl.pallas_call(
        functools.partial(
            hidden_grad_kernel, half, tuple(len(s) for s in streams), tile, partial is not None, by is not None
        ),
        grid=(ff // tile,),
        in_specs=in_specs,
        out_specs=out_specs,
        scratch_shapes=scratch,
        out_shape=out_shape,
        input_output_aliases=aliases,
        cost_estimate=pl.CostEstimate(
            flops=2 * rows * ff * sum(w.shape[1] for w in weights), bytes_accessed=12 * rows * ff, transcendentals=0
        ),
        compiler_params=pltpu.CompilerParams(vmem_limit_bytes=VMEM_LIMIT),
        name="hidden_grad_" + half + ("" if by is not None else "_partial"),
    )(*args)


def weight_grad_kernel(n, *refs):
    hidden, block, send, keep = refs[:n], refs[n], refs[n + 1], refs[n + 2]
    half = send.shape[1]
    lhs = jnp.concatenate([h[...] for h in hidden], axis=0) if n > 1 else hidden[0][...]
    total = contract_first(lhs, block[...]).astype(BF16)
    core = lax.axis_index("dp") % 2

    @pl.when(core == 0)
    def _():
        keep[...] = total[:, :half]
        send[...] = total[:, half:]

    @pl.when(core == 1)
    def _():
        send[...] = total[:, :half]
        keep[...] = total[:, half:]


def weight_grad(block, hiddens):
    (tok, ff), half = hiddens[0].shape, block.shape[1] // 2
    tile = pick_tile(ff, 256)
    return pl.pallas_call(
        functools.partial(weight_grad_kernel, len(hiddens)),
        grid=(ff // tile,),
        in_specs=[pl.BlockSpec((tok, tile), lambda i: (0, i))] * len(hiddens) + [VMEM_SPEC],
        out_specs=[pl.BlockSpec((tile, half), lambda i: (i, 0))] * 2,
        out_shape=[pltpu.HBM((ff, half), BF16)] * 2,
        cost_estimate=pl.CostEstimate(
            flops=4 * block.shape[0] * ff * half, bytes_accessed=2 * ff * (block.shape[0] + 2 * half), transcendentals=0
        ),
        compiler_params=pltpu.CompilerParams(vmem_limit_bytes=VMEM_LIMIT),
        name="weight_grad",
    )(*in_hbm(hiddens), in_vmem(block))


def add_kernel(scale, a_ref, b_ref, *refs):
    refs[-1][...] = ((a_ref[...].astype(F32) + b_ref[...].astype(F32)) * scale).astype(BF16)


def add_rows(keep, got, scale, row, total_rows, out=None):
    rows, cols = keep.shape
    tile = pick_tile(math.gcd(rows, row), 512)
    first = row // tile
    spec = pl.BlockSpec((tile, cols), lambda i: (i, 0))
    in_specs, args, aliases = [spec, spec], [keep, got], {}
    if out is not None:
        aliases = {2: 0}
        in_specs.append(ANY_SPEC)
        args += in_hbm([out])
    return pl.pallas_call(
        functools.partial(add_kernel, scale),
        grid=(rows // tile,),
        in_specs=in_specs,
        out_specs=pl.BlockSpec((tile, cols), lambda i: (i + first, 0)),
        out_shape=pltpu.HBM((total_rows, cols), BF16),
        input_output_aliases=aliases,
        cost_estimate=pl.CostEstimate(flops=2 * rows * cols, bytes_accessed=6 * rows * cols, transcendentals=0),
        compiler_params=pltpu.CompilerParams(vmem_limit_bytes=VMEM_LIMIT),
        name="add_rows",
    )(*args)


def on_device(out_grad, gate_pre, up_pre, down_weight):
    grad, gate, up = out_grad[0], gate_pre[0], up_pre[0]
    tok, ff = gate.shape
    d = grad.shape[1]
    dp, nt = lax.axis_size("dp"), lax.axis_size("tensor")
    chips = dp // 2
    cols = d // chips
    chip, pair = lax.axis_index("dp") // 2, lax.axis_index("tensor") // 2
    scale = 1.0 / math.sqrt(tok * dp)

    def shift(value, s):
        return lax.ppermute(
            value, "dp", [(2 * c + k, 2 * ((c + s) % chips) + k) for c in range(chips) for k in range(2)]
        )

    def swap_cores(value):
        return lax.ppermute(value, "dp", [(k, k ^ 1) for k in range(dp)])

    def columns_of(which):
        return lax.dynamic_slice(grad, (0, which * cols), (grad.shape[0], cols))

    if nt == 4 and chips == 2 and ff % 896 == 0:
        cut = 5 * ff // 7
        both_ways = lambda *pairs: [q for a, b in pairs for q in ((a, b), (b, a))]
        swap_pair = lambda v: lax.ppermute(v, "tensor", both_ways((0, 1), (2, 3)))
        swap_middle = lambda v: lax.ppermute(v, "tensor", both_ways((1, 2)))
        to_ends = lambda v: lax.ppermute(v, "tensor", [(1, 0), (2, 3)])

        mine, rest = together(columns_of(chip), columns_of(1 - chip))
        far = shift(rest, 1)
        a1, b01 = swap_pair(mine), swap_middle(mine)
        (h0,) = factors(hidden_kernel, gate, up, cut, [cut])
        a1, b01, rest = together(a1, b01, rest)
        c01, b11 = to_ends(b01), swap_middle(a1)
        a2, b02 = swap_pair(rest), swap_middle(rest)

        far, h0, gate, up = together(far, h0, gate, up)
        h0_in = shift(h0, 1)
        a3, b03 = swap_pair(far), swap_middle(far)
        h1, *by = factors(functools.partial(factors_kernel, cut), gate, up, ff, [ff - cut, ff, ff])

        a2, h1, by, weight = together(a2, h1, by, down_weight)
        h1_in = shift(h1, 1)
        *weights, mark = load_weight(weight, chips)

        b11, mark = together(b11, mark)
        c11 = to_ends(b11)
        outs = hidden_grad("early", [[mine, a1], [rest, a2]], weights, tok, None, by)

        a3, b03, outs = together(a3, b03, outs)
        c03, b13 = to_ends(b03), swap_middle(a3)
        b13, c01, c11, a2, b02 = together(b13, c01, c11, a2, b02)
        c13, b12, c02 = to_ends(b13), swap_middle(a2), to_ends(b02)
        block = in_token_order([mine, a1, b01, b11, c01, c11])
        partial = hidden_grad("late", [[b01, b11, c01, c11]], weights[:1], tok)

        b12, partial = together(b12, partial)
        c12 = to_ends(b12)
        c03, c13, h0_in, partial = together(c03, c13, h0_in, partial)
        block = in_token_order([far, a3, b03, b13, c03, c13], [block])
        send0, keep0 = weight_grad(block, [h0, h0_in])
        send0, keep0, h1, h1_in = together(send0, keep0, h1, h1_in)
        got0 = swap_cores(send0)
        send1, keep1 = weight_grad(block, [h1, h1_in])
        send1, keep1, got0 = together(send1, keep1, got0)
        got1 = swap_cores(send1)
        down_grad = add_rows(keep0, got0, scale, 0, ff)
        c02, c12, down_grad, partial = together(c02, c12, down_grad, partial)
        outs = hidden_grad("late", [[b02, b12, c02, c12]], weights[1:], tok, partial, by, outs)
        got1, outs = together(got1, outs)
        down_grad = add_rows(keep1, got1, scale, cut, ff, down_grad)
    else:
        gather = lambda v: lax.all_gather(v, "tensor", axis=0, tiled=True)
        hidden, *by = factors(functools.partial(factors_kernel, 0), gate, up, ff, [ff, ff, ff])
        hiddens = [hidden] + [shift(hidden, s) for s in range(1, chips)]
        blocks = [gather(columns_of(chip))]
        blocks += [gather(shift(columns_of((chip + s) % chips), s)) for s in range(1, chips)]
        block = jnp.concatenate(blocks, axis=0)
        outs = hidden_grad("all", [[gather(grad)]], load_weight(down_weight, 1)[:1], tok, None, by)
        send, keep = weight_grad(block, hiddens)
        down_grad = add_rows(keep, swap_cores(send), scale, 0, ff)
    return (outs[0][None], outs[1][None], down_grad)


def solution(mesh):
    return jax.shard_map(
        on_device,
        mesh=mesh,
        in_specs=(
            P("dp", ("groups", "tensor"), None),
            P("dp", "groups", "tensor"),
            P("dp", "groups", "tensor"),
            P("tensor", None),
        ),
        out_specs=(
            P("dp", "groups", "tensor"),
            P("dp", "groups", "tensor"),
            P(("groups", "tensor"), "dp"),
        ),
        check_vma=False,
    )
```

```python
import functools
import math

import jax
import jax.numpy as jnp
from jax import lax
from jax.experimental import pallas as pl
from jax.experimental.pallas import tpu as pltpu
from jax.sharding import PartitionSpec as P

VMEM_LIMIT = 10 * 1024 * 1024
F32, BF16 = jnp.float32, jnp.bfloat16
SHORT = pl.CostEstimate(flops=1, bytes_accessed=1, transcendentals=0)
LONG = pl.CostEstimate(flops=10**12, bytes_accessed=10**9, transcendentals=0)
ANY_SPEC = pl.BlockSpec(memory_space=pl.ANY)
VMEM_SPEC = pl.BlockSpec(memory_space=pltpu.VMEM)


def pick_tile(extent, cap):
    return max(t for t in range(128, cap + 1, 128) if extent % t == 0)


def together(*values):
    return lax.optimization_barrier(values)


def sigmoid(x):
    return 0.5 + 0.5 * jnp.tanh(0.5 * x)


def contract_last(a, b):
    return lax.dot_general(a, b, (((1,), (1,)), ((), ())), preferred_element_type=F32)


def contract_first(a, b):
    return lax.dot_general(a, b, (((0,), (0,)), ((), ())), preferred_element_type=F32)


def in_vmem(value):
    return pltpu.with_memory_space_constraint(value, pltpu.VMEM)


def in_hbm(values):
    return [pltpu.with_memory_space_constraint(v, pltpu.HBM) for v in values]


def place_shards(parts, half, into, sem, start, by_core=False):
    act = (lambda c: c.start()) if start else (lambda c: c.wait())
    z = lax.axis_index("tensor")
    pair = z // 2
    parts = list(parts)
    slot = iter(range(16))

    def place(ref, row):
        rows = ref.shape[0]
        at = pl.ds(pl.multiple_of(row, 16), rows)
        if not by_core:
            act(pltpu.make_async_copy(ref, into.at[at], sem.at[next(slot)]))
            return
        cols = ref.shape[1] // 2
        for k in range(2):
            there = pl.multiple_of(jnp.where(lax.axis_index("dp") % 2 == k, 1, 0) * cols, cols)
            copy = pltpu.make_async_copy(
                ref.at[:, pl.ds(k * cols, cols)], into.at[at, pl.ds(there, cols)], sem.at[next(slot)]
            )
            act(copy)

    if half != "late":
        whole = parts[0].shape[0] * (2 if half == "early" else 4) == into.shape[0]
        base = 0 if half == "early" else pair * (into.shape[0] // 2)
        if whole:
            rows = parts[0].shape[0]
            place(parts.pop(0), base + (z % 2) * rows)
            place(parts.pop(0), base + (1 - z % 2) * rows)
        else:
            place(parts.pop(0), base)
    if half != "early":
        base = 0 if half == "late" else (1 - pair) * (into.shape[0] // 2)
        middle = jnp.logical_or(z == 1, z == 2)
        rows = parts[0].shape[0]
        steps = [base] if len(parts) == 2 else [base + pair * rows, base + (1 - pair) * rows]
        n = len(parts) // 2

        @pl.when(middle)
        def _():
            for ref, row in zip(parts[:n], steps):
                place(ref, row)

        @pl.when(jnp.logical_not(middle))
        def _():
            for ref, row in zip(parts[n:], steps):
                place(ref, row)


def move_kernel(half, by_core, n_parts, *refs):
    parts, (into, sem) = refs[:n_parts], refs[-2:]
    for start in (True, False):
        place_shards(parts, half, into, sem, start, by_core)


def in_token_order(half, rows, parts, by_core=False, wait_for=()):
    cols = parts[0].shape[1]
    return pl.pallas_call(
        functools.partial(move_kernel, half, by_core, len(parts)),
        in_specs=[ANY_SPEC] * (len(parts) + len(wait_for)),
        out_specs=VMEM_SPEC,
        out_shape=pltpu.VMEM((rows, cols), BF16),
        scratch_shapes=[pltpu.SemaphoreType.DMA((16,))],
        compiler_params=pltpu.CompilerParams(vmem_limit_bytes=VMEM_LIMIT),
        name="in_token_order",
    )(*parts, *wait_for)


def mark_kernel(*refs):
    out = refs[-1]
    out[...] = jnp.zeros(out.shape, out.dtype)


def mark_of(values, cost):
    return pl.pallas_call(
        mark_kernel,
        in_specs=[ANY_SPEC] * len(values),
        out_specs=VMEM_SPEC,
        out_shape=jax.ShapeDtypeStruct((8, 128), F32),
        cost_estimate=pl.CostEstimate(flops=1, bytes_accessed=cost, transcendentals=0),
        compiler_params=pltpu.CompilerParams(vmem_limit_bytes=VMEM_LIMIT),
        name="mark",
    )(*values)


def load_weight_kernel(weight, *refs):
    outs, mark, sem = refs[:-2], refs[-2], refs[-1]
    chip = lax.axis_index("dp") // 2
    copies = []
    for s, out in enumerate(outs):
        width = out.shape[1]
        at = pl.multiple_of(lax.rem(chip + s, len(outs)) * width, width)
        copies.append(pltpu.make_async_copy(weight.at[:, pl.ds(at, width)], out, sem.at[s]))
    for copy in copies:
        copy.start()
    mark[...] = jnp.zeros(mark.shape, mark.dtype)
    for copy in copies:
        copy.wait()


def load_weight(weight, blocks):
    ff, d = weight.shape
    return pl.pallas_call(
        load_weight_kernel,
        in_specs=[ANY_SPEC],
        out_specs=[VMEM_SPEC] * (blocks + 1),
        out_shape=[pltpu.VMEM((ff, d // blocks), BF16)] * blocks + [jax.ShapeDtypeStruct((8, 128), F32)],
        scratch_shapes=[pltpu.SemaphoreType.DMA((blocks,))],
        cost_estimate=LONG,
        compiler_params=pltpu.CompilerParams(vmem_limit_bytes=VMEM_LIMIT),
        name="load_weight",
    )(*in_hbm([weight]))


def hidden_kernel(gate_ref, up_ref, *hidden_refs):
    at = 0
    for ref in hidden_refs:
        columns = slice(at, at + ref.shape[1])
        gate, up = gate_ref[:, columns].astype(F32), up_ref[:, columns].astype(F32)
        ref[...] = (gate * sigmoid(gate) * up).astype(BF16)
        at += ref.shape[1]


def hidden_chunks(gate, up, widths):
    tok, ff = gate.shape
    rows = next(r for r in (64, 32, 16) if tok % r == 0)
    spec = lambda w: pl.BlockSpec((rows, w), lambda i: (i, 0))
    return pl.pallas_call(
        hidden_kernel,
        grid=(tok // rows,),
        in_specs=[spec(ff)] * 2,
        out_specs=[spec(w) for w in widths],
        out_shape=[pltpu.HBM((tok, w), BF16) for w in widths],
        cost_estimate=SHORT,
        compiler_params=pltpu.CompilerParams(vmem_limit_bytes=VMEM_LIMIT),
        name="hidden",
    )(*in_hbm([gate, up]))


def hidden_grad_kernel(half, counts, tile, has_partial, finish, *refs):
    refs = list(refs)
    streams = [[refs.pop(0) for _ in range(count)] for count in counts]
    weights = [refs.pop(0) for _ in counts]
    partial = refs.pop(0) if has_partial else None
    if sum(counts) == len(counts):
        lhs = [stream[0] for stream in streams]
    else:
        sem = refs.pop()
        lhs = refs[-len(counts) :]
        refs = refs[: -len(counts)]

        @pl.when(pl.program_id(0) == 0)
        def _():
            for start in (True, False):
                for s, parts in enumerate(streams):
                    place_shards(parts, half, lhs[s], sem.at[s], start)

    step = pl.program_id(0)
    at = pl.multiple_of(step * tile, tile)
    total = partial[...] if has_partial else None
    for left, weight in zip(lhs, weights):
        term = contract_last(left[...], weight[pl.ds(at, tile), :])
        total = term if total is None else total + term
    if not finish:
        refs[-1][...] = total
        return
    gate, up = refs[0][...].astype(F32), refs[1][...].astype(F32)
    gate_out, up_out = refs[-2:]
    sig = sigmoid(gate)
    gate_out[...] = (total * up * sig * (1.0 + gate * (1.0 - sig))).astype(BF16)
    up_out[...] = (total * (gate * sig)).astype(BF16)


def hidden_grad(half, streams, weights, tok, partial=None, by=None, outs=None, wait_for=()):
    ff = weights[0].shape[0]
    rows = tok if half == "all" else tok // 2
    tile = pick_tile(ff, 896 if by is None else 512)

    def place(i):
        pair = lax.axis_index("tensor") // 2
        return ({"all": 0, "early": pair, "late": 1 - pair}[half], i)

    block = pl.BlockSpec((rows, tile), place)
    part_block = pl.BlockSpec((rows, tile), lambda i: (0, i))
    if all(len(s) == 1 for s in streams):
        in_specs, args, scratch = [VMEM_SPEC] * len(streams), [in_vmem(s[0]) for s in streams], []
    else:
        args = [part for s in streams for part in s]
        in_specs = [ANY_SPEC] * len(args)
        scratch = [pltpu.VMEM((rows, w.shape[1]), BF16) for w in weights] + [
            pltpu.SemaphoreType.DMA((len(weights), 16))
        ]
    in_specs += [VMEM_SPEC] * len(weights)
    args += [in_vmem(w) for w in weights]
    aliases = {}
    if partial is not None:
        in_specs.append(part_block)
        args += in_hbm([partial])
    if by is not None:
        in_specs += [block] * 2
        args += in_hbm(by)
    in_specs += [ANY_SPEC] * len(wait_for)
    args += wait_for
    if by is not None:
        out_shape, out_specs = [pltpu.HBM((tok, ff), BF16)] * 2, [block] * 2
        if outs is not None:
            aliases = {len(args): 0, len(args) + 1: 1}
            in_specs += [ANY_SPEC] * 2
            args += in_hbm(outs)
    else:
        out_shape, out_specs = pltpu.HBM((rows, ff), F32), part_block
    return pl.pallas_call(
        functools.partial(
            hidden_grad_kernel,
            half,
            tuple(len(s) for s in streams),
            tile,
            partial is not None,
            by is not None,
        ),
        grid=(ff // tile,),
        in_specs=in_specs,
        out_specs=out_specs,
        scratch_shapes=scratch,
        out_shape=out_shape,
        input_output_aliases=aliases,
        cost_estimate=LONG if outs is not None else SHORT,
        compiler_params=pltpu.CompilerParams(vmem_limit_bytes=VMEM_LIMIT),
        name="hidden_grad_" + half + ("" if by is not None else "_partial"),
    )(*args)


def weight_grad_kernel(tile, has_start, split, hidden, block, *refs):
    at = pl.ds(pl.multiple_of(pl.program_id(0) * tile, tile), tile)
    total = contract_first(hidden[...], block[...])
    if has_start:
        total = total + refs[0][at, :].astype(F32)
    total = total.astype(BF16)
    if not split:
        refs[-1][at, :] = total
        return
    send, keep = refs[-2:]
    half = send.shape[1]
    send[...] = total[:, :half]
    keep[...] = total[:, half:]


def weight_grad(block, hidden, start=None, split=True):
    (tok, ff), cols = hidden.shape, block.shape[1]
    tile = pick_tile(ff, 256)
    in_specs = [pl.BlockSpec((tok, tile), lambda i: (0, i)), VMEM_SPEC]
    args = [hidden, in_vmem(block)]
    if start is not None:
        in_specs.append(VMEM_SPEC)
        args.append(in_vmem(start))
    if split:
        out_specs = [pl.BlockSpec((tile, cols // 2), lambda i: (i, 0))] * 2
        out_shape = [pltpu.HBM((ff, cols // 2), BF16), jax.ShapeDtypeStruct((ff, cols // 2), BF16)]
    else:
        out_specs, out_shape = VMEM_SPEC, pltpu.VMEM((ff, cols), BF16)
    return pl.pallas_call(
        functools.partial(weight_grad_kernel, tile, start is not None, split),
        grid=(ff // tile,),
        in_specs=in_specs,
        out_specs=out_specs,
        out_shape=out_shape,
        cost_estimate=SHORT,
        compiler_params=pltpu.CompilerParams(vmem_limit_bytes=VMEM_LIMIT),
        name="weight_grad",
    )(*args)


def add_kernel(scale, a_ref, b_ref, *refs):
    refs[-1][...] = ((a_ref[...].astype(F32) + b_ref[...].astype(F32)) * scale).astype(BF16)


def add_rows(keep, got, scale, row, total_rows, out=None):
    rows, cols = keep.shape
    tile = pick_tile(math.gcd(rows, row), 512)
    first = row // tile
    spec = pl.BlockSpec((tile, cols), lambda i: (i, 0))
    in_specs, args, aliases = [spec] * 2, [keep, got], {}
    if out is not None:
        aliases = {2: 0}
        in_specs.append(ANY_SPEC)
        args += in_hbm([out])
    return pl.pallas_call(
        functools.partial(add_kernel, scale),
        grid=(rows // tile,),
        in_specs=in_specs,
        out_specs=pl.BlockSpec((tile, cols), lambda i: (i + first, 0)),
        out_shape=pltpu.HBM((total_rows, cols), BF16),
        input_output_aliases=aliases,
        cost_estimate=SHORT,
        compiler_params=pltpu.CompilerParams(vmem_limit_bytes=VMEM_LIMIT),
        name="add_rows",
    )(*args)


def on_device(out_grad, gate_pre, up_pre, down_weight):
    grad, gate, up = out_grad[0], gate_pre[0], up_pre[0]
    tok, ff = gate.shape
    d = grad.shape[1]
    dp, nt = lax.axis_size("dp"), lax.axis_size("tensor")
    chips = dp // 2
    cols = d // chips
    chip, pair = lax.axis_index("dp") // 2, lax.axis_index("tensor") // 2
    scale = 1.0 / math.sqrt(tok * dp)

    def shift(value, s):
        return lax.ppermute(
            value, "dp", [(2 * c + k, 2 * ((c + s) % chips) + k) for c in range(chips) for k in range(2)]
        )

    def swap_cores(value):
        return lax.ppermute(value, "dp", [(k, k ^ 1) for k in range(dp)])

    def columns_of(which):
        return lax.dynamic_slice(grad, (0, which * cols), (grad.shape[0], cols))

    if nt == 4 and chips == 2 and ff % 896 == 0:
        cut = 6 * ff // 7
        both_ways = lambda *pairs: [q for a, b in pairs for q in ((a, b), (b, a))]
        swap_pair = lambda v: lax.ppermute(v, "tensor", both_ways((0, 1), (2, 3)))
        swap_middle = lambda v: lax.ppermute(v, "tensor", both_ways((1, 2)))
        to_ends = lambda v: lax.ppermute(v, "tensor", [(1, 0), (2, 3)])

        mine, rest = together(columns_of(chip), columns_of(1 - chip))
        far, a1 = shift(rest, 1), swap_pair(mine)
        h0, h1 = hidden_chunks(gate, up, [cut, ff - cut])
        far, h0 = together(far, h0)
        a1, rest, first, weight, h1 = together(a1, rest, mark_of([far], 10**6), down_weight, h1)

        h0_in = shift(h0, 1)
        a3, a2 = swap_pair(far), swap_pair(rest)
        pair1 = in_token_order("early", tok // 2, [mine, a1], wait_for=[first])
        b1 = swap_middle(pair1)
        *weights, mark = load_weight(weight, chips)
        a3, mark = together(a3, mark)

        pair3 = in_token_order("early", tok // 2, [far, a3], wait_for=[mark])
        b3 = swap_middle(pair3)
        b1, a2 = together(b1, a2)

        c1 = to_ends(b1)
        pair2 = in_token_order("early", tok // 2, [rest, a2])
        outs = hidden_grad("early", [[pair1], [pair2]], weights, tok, None, (gate, up))
        b3, c1, outs, pair2, h1 = together(b3, c1, outs, pair2, h1)

        c3, b2 = to_ends(b3), swap_middle(pair2)
        h1_in = shift(h1, 1)
        partial = hidden_grad("late", [[b1, c1]], weights[:1], tok)
        h0, h1, partial = together(h0, h1, partial)
        block = in_token_order("all", tok, [pair1, b1, c1], by_core=True)
        own0, own1 = weight_grad(block, h0, split=False), weight_grad(block, h1, split=False)
        first = mark_of([own0, own1], 1)
        b2, partial, first = together(b2, partial, first)

        c2 = to_ends(b2)
        c3, h0_in, partial, first = together(c3, h0_in, partial, first)
        block = in_token_order("all", tok, [pair3, b3, c3], by_core=True, wait_for=[first])
        send0, keep0 = weight_grad(block, h0_in, own0)
        got0 = swap_cores(send0)
        send0, h1_in = together(send0, h1_in)
        send1, keep1 = weight_grad(block, h1_in, own1)
        got1 = swap_cores(send1)
        c2, send1, partial = together(c2, send1, partial)
        outs = hidden_grad("late", [[b2, c2]], weights[1:], tok, partial, (gate, up), outs, [send1])
        got0, got1, outs = together(got0, got1, outs)
        down_grad = add_rows(keep0, got0, scale, 0, ff)
        down_grad = add_rows(keep1, got1, scale, cut, ff, down_grad)
    else:
        gather = lambda v: lax.all_gather(v, "tensor", axis=0, tiled=True)
        (hidden,) = hidden_chunks(gate, up, [ff])
        hiddens = [hidden] + [shift(hidden, s) for s in range(1, chips)]

        def by_core(value):
            return jnp.where(lax.axis_index("dp") % 2 == 0, jnp.roll(value, cols // 2, axis=1), value)

        blocks = [by_core(gather(columns_of(chip)))]
        blocks += [by_core(gather(shift(columns_of((chip + s) % chips), s))) for s in range(1, chips)]
        total = None
        for block, part in zip(blocks[:-1], hiddens[:-1]):
            total = weight_grad(block, part, total, split=False)
        send, keep = weight_grad(blocks[-1], hiddens[-1], total)
        outs = hidden_grad("all", [[gather(grad)]], load_weight(down_weight, 1)[:1], tok, None, (gate, up))
        down_grad = add_rows(keep, swap_cores(send), scale, 0, ff)
    return (outs[0][None], outs[1][None], down_grad)


def solution(mesh):
    return jax.shard_map(
        on_device,
        mesh=mesh,
        in_specs=(
            P("dp", ("groups", "tensor"), None),
            P("dp", "groups", "tensor"),
            P("dp", "groups", "tensor"),
            P("tensor", None),
        ),
        out_specs=(
            P("dp", "groups", "tensor"),
            P("dp", "groups", "tensor"),
            P(("groups", "tensor"), "dp"),
        ),
        check_vma=False,
    )
```

```python
import functools
import math

import jax
import jax.numpy as jnp
from jax import lax
from jax.experimental import pallas as pl
from jax.experimental.pallas import tpu as pltpu
from jax.sharding import PartitionSpec as P

VMEM_LIMIT = 10 * 1024 * 1024
F32, BF16 = jnp.float32, jnp.bfloat16
SHORT = pl.CostEstimate(flops=1, bytes_accessed=1, transcendentals=0)
BRIEF = pl.CostEstimate(flops=1, bytes_accessed=10**6, transcendentals=0)
LONG = pl.CostEstimate(flops=10**12, bytes_accessed=10**9, transcendentals=0)
ANY_SPEC = pl.BlockSpec(memory_space=pl.ANY)
VMEM_SPEC = pl.BlockSpec(memory_space=pltpu.VMEM)


def pick_tile(extent, cap):
    return max(t for t in range(128, cap + 1, 128) if extent % t == 0)


def together(*values):
    return lax.optimization_barrier(values)


def sigmoid(x):
    return 0.5 + 0.5 * jnp.tanh(0.5 * x)


def contract_last(a, b):
    return lax.dot_general(a, b, (((1,), (1,)), ((), ())), preferred_element_type=F32)


def contract_first(a, b):
    return lax.dot_general(a, b, (((0,), (0,)), ((), ())), preferred_element_type=F32)


def in_vmem(value):
    return pltpu.with_memory_space_constraint(value, pltpu.VMEM)


def in_hbm(values):
    return [pltpu.with_memory_space_constraint(v, pltpu.HBM) for v in values]


def place_shards(parts, half, into, sem, start, by_core=False, swapped_from=0):
    act = (lambda c: c.start()) if start else (lambda c: c.wait())
    z = lax.axis_index("tensor")
    pair = z // 2
    parts = list(parts)
    slot = iter(range(16))

    def place(ref, row):
        rows = ref.shape[0]
        at = pl.ds(pl.multiple_of(row, 16), rows)
        if not by_core:
            act(pltpu.make_async_copy(ref, into.at[at], sem.at[next(slot)]))
            return
        cols = ref.shape[1] // 2
        for k in range(2):
            there = pl.multiple_of(jnp.where(lax.axis_index("dp") % 2 == k, 1, 0) * cols, cols)
            copy = pltpu.make_async_copy(
                ref.at[:, pl.ds(k * cols, cols)], into.at[at, pl.ds(there, cols)], sem.at[next(slot)]
            )
            act(copy)

    if half != "late":
        whole = parts[0].shape[0] * (2 if half == "early" else 4) == into.shape[0]
        base = 0 if half == "early" else pair * (into.shape[0] // 2)
        if whole:
            rows = parts[0].shape[0]
            place(parts.pop(0), base + (z % 2) * rows)
            place(parts.pop(0).at[pl.ds(swapped_from, rows)], base + (1 - z % 2) * rows)
        else:
            place(parts.pop(0), base)
    if half != "early":
        base = 0 if half == "late" else (1 - pair) * (into.shape[0] // 2)
        middle = jnp.logical_or(z == 1, z == 2)
        if len(parts) == 3:
            place(parts[2], base + parts[0].shape[0])

        @pl.when(middle)
        def _():
            place(parts[0], base)

        @pl.when(jnp.logical_not(middle))
        def _():
            place(parts[1], base)


def move_kernel(half, by_core, swapped_from, n_parts, *refs):
    parts, (into, sem) = refs[:n_parts], refs[-2:]
    for start in (True, False):
        place_shards(parts, half, into, sem, start, by_core, swapped_from)


def in_token_order(half, rows, parts, by_core=False, swapped_from=0, wait_for=(), cost=None):
    cols = parts[0].shape[1]
    return pl.pallas_call(
        functools.partial(move_kernel, half, by_core, swapped_from, len(parts)),
        in_specs=[ANY_SPEC] * (len(parts) + len(wait_for)),
        out_specs=VMEM_SPEC,
        out_shape=pltpu.VMEM((rows, cols), BF16),
        scratch_shapes=[pltpu.SemaphoreType.DMA((16,))],
        cost_estimate=cost,
        compiler_params=pltpu.CompilerParams(vmem_limit_bytes=VMEM_LIMIT),
        name="in_token_order",
    )(*parts, *in_hbm(wait_for))


def stack_kernel(*refs):
    parts, into, sem = refs[:-2], refs[-2], refs[-1]
    copies = []
    for k, part in enumerate(parts):
        rows = part.shape[0]
        copies.append(pltpu.make_async_copy(part, into.at[pl.ds(k * rows, rows)], sem.at[k]))
    for copy in copies:
        copy.start()
    for copy in copies:
        copy.wait()


def stack(parts):
    rows, cols = parts[0].shape
    return pl.pallas_call(
        stack_kernel,
        in_specs=[ANY_SPEC] * len(parts),
        out_specs=VMEM_SPEC,
        out_shape=pltpu.VMEM((rows * len(parts), cols), BF16),
        scratch_shapes=[pltpu.SemaphoreType.DMA((len(parts),))],
        compiler_params=pltpu.CompilerParams(vmem_limit_bytes=VMEM_LIMIT),
        name="stack",
    )(*parts)


def take_rows_kernel(row, *refs):
    parts, out, sem = refs[:-2], refs[-2], refs[-1]
    z = lax.axis_index("tensor")
    middle = jnp.logical_or(z == 1, z == 2)
    here = [None] if len(parts) == 1 else [middle, jnp.logical_not(middle)]

    def take(part):
        copy = pltpu.make_async_copy(part.at[pl.ds(row, out.shape[0])], out, sem)
        copy.start()
        copy.wait()

    for part, condition in zip(parts, here):
        if condition is None:
            take(part)
        else:
            pl.when(condition)(functools.partial(take, part))


def take_rows(parts, row, rows):
    return pl.pallas_call(
        functools.partial(take_rows_kernel, row),
        in_specs=[ANY_SPEC] * len(parts),
        out_specs=VMEM_SPEC,
        out_shape=pltpu.VMEM((rows, parts[0].shape[1]), BF16),
        scratch_shapes=[pltpu.SemaphoreType.DMA],
        compiler_params=pltpu.CompilerParams(vmem_limit_bytes=VMEM_LIMIT),
        name="take_rows",
    )(*parts)


def mark_kernel(*refs):
    out = refs[-1]
    out[...] = jnp.zeros(out.shape, out.dtype)


def mark_of(values, cost):
    return pl.pallas_call(
        mark_kernel,
        in_specs=[ANY_SPEC] * len(values),
        out_specs=pl.BlockSpec((8, 128), lambda: (0, 0)),
        out_shape=pltpu.HBM((8, 128), F32),
        cost_estimate=pl.CostEstimate(flops=1, bytes_accessed=cost, transcendentals=0),
        compiler_params=pltpu.CompilerParams(vmem_limit_bytes=VMEM_LIMIT),
        name="mark",
    )(*values)


def load_weight_kernel(weight, *refs):
    outs, mark, sem = refs[:-2], refs[-2], refs[-1]
    chip = lax.axis_index("dp") // 2
    copies = []
    for s, out in enumerate(outs):
        width = out.shape[1]
        at = pl.multiple_of(lax.rem(chip + s, len(outs)) * width, width)
        copies.append(pltpu.make_async_copy(weight.at[:, pl.ds(at, width)], out, sem.at[s]))
    for copy in copies:
        copy.start()
    mark[...] = jnp.zeros(mark.shape, mark.dtype)
    for copy in copies:
        copy.wait()


def load_weight(weight, blocks):
    ff, d = weight.shape
    return pl.pallas_call(
        load_weight_kernel,
        in_specs=[ANY_SPEC],
        out_specs=[VMEM_SPEC] * blocks + [pl.BlockSpec((8, 128), lambda: (0, 0))],
        out_shape=[pltpu.VMEM((ff, d // blocks), BF16)] * blocks + [pltpu.HBM((8, 128), F32)],
        scratch_shapes=[pltpu.SemaphoreType.DMA((blocks,))],
        cost_estimate=SHORT,
        compiler_params=pltpu.CompilerParams(vmem_limit_bytes=VMEM_LIMIT),
        name="load_weight",
    )(*in_hbm([weight]))


def hidden_kernel(gate_ref, up_ref, hidden_ref):
    gate, up = gate_ref[...].astype(F32), up_ref[...].astype(F32)
    hidden_ref[...] = (gate * sigmoid(gate) * up).astype(BF16)


def hidden_of(gate, up):
    tok, ff = gate.shape
    rows = next(r for r in (64, 32, 16) if tok % r == 0)
    spec = pl.BlockSpec((rows, ff), lambda i: (i, 0))
    return pl.pallas_call(
        hidden_kernel,
        grid=(tok // rows,),
        in_specs=[spec] * 2,
        out_specs=spec,
        out_shape=pltpu.HBM((tok, ff), BF16),
        cost_estimate=SHORT,
        compiler_params=pltpu.CompilerParams(vmem_limit_bytes=VMEM_LIMIT),
        name="hidden",
    )(*in_hbm([gate, up]))


def hidden_grad_kernel(half, counts, tile, has_partial, finish, *refs):
    refs = list(refs)
    streams = [[refs.pop(0) for _ in range(count)] for count in counts]
    weights = [refs.pop(0) for _ in counts]
    partial = refs.pop(0) if has_partial else None
    if sum(counts) == len(counts):
        lhs = [stream[0] for stream in streams]
    else:
        sem = refs.pop()
        lhs = refs[-len(counts) :]
        refs = refs[: -len(counts)]

        @pl.when(pl.program_id(0) == 0)
        def _():
            for start in (True, False):
                for s, parts in enumerate(streams):
                    place_shards(parts, half, lhs[s], sem.at[s], start)

    step = pl.program_id(0)
    at = pl.multiple_of(step * tile, tile)
    total = partial[...] if has_partial else None
    for left, weight in zip(lhs, weights):
        term = contract_last(left[...], weight[pl.ds(at, tile), :])
        total = term if total is None else total + term
    if not finish:
        refs[-1][...] = total
        return
    gate, up = refs[0][...].astype(F32), refs[1][...].astype(F32)
    gate_out, up_out = refs[-2:]
    sig = sigmoid(gate)
    gate_out[...] = (total * up * sig * (1.0 + gate * (1.0 - sig))).astype(BF16)
    up_out[...] = (total * (gate * sig)).astype(BF16)


def hidden_grad(half, streams, weights, tok, partial=None, by=None, outs=None, wait_for=()):
    ff = weights[0].shape[0]
    rows = tok if half == "all" else tok // 2
    tile = pick_tile(ff, 896 if by is None else 512)

    def place(i):
        pair = lax.axis_index("tensor") // 2
        return ({"all": 0, "early": pair, "late": 1 - pair}[half], i)

    block = pl.BlockSpec((rows, tile), place)
    part_block = pl.BlockSpec((rows, tile), lambda i: (0, i))
    if all(len(s) == 1 for s in streams):
        in_specs, args, scratch = [VMEM_SPEC] * len(streams), [in_vmem(s[0]) for s in streams], []
    else:
        args = [part for s in streams for part in s]
        in_specs = [ANY_SPEC] * len(args)
        scratch = [pltpu.VMEM((rows, w.shape[1]), BF16) for w in weights] + [
            pltpu.SemaphoreType.DMA((len(weights), 16))
        ]
    in_specs += [VMEM_SPEC] * len(weights)
    args += [in_vmem(w) for w in weights]
    aliases = {}
    if partial is not None:
        in_specs.append(part_block)
        args += in_hbm([partial])
    if by is not None:
        in_specs += [block] * 2
        args += in_hbm(by)
    in_specs += [ANY_SPEC] * len(wait_for)
    args += in_hbm(wait_for)
    if by is not None:
        out_shape, out_specs = [pltpu.HBM((tok, ff), BF16)] * 2, [block] * 2
        if outs is not None:
            aliases = {len(args): 0, len(args) + 1: 1}
            in_specs += [ANY_SPEC] * 2
            args += in_hbm(outs)
    else:
        out_shape, out_specs = pltpu.HBM((rows, ff), F32), part_block
    return pl.pallas_call(
        functools.partial(
            hidden_grad_kernel,
            half,
            tuple(len(s) for s in streams),
            tile,
            partial is not None,
            by is not None,
        ),
        grid=(ff // tile,),
        in_specs=in_specs,
        out_specs=out_specs,
        scratch_shapes=scratch,
        out_shape=out_shape,
        input_output_aliases=aliases,
        cost_estimate=LONG if outs is not None else SHORT,
        compiler_params=pltpu.CompilerParams(vmem_limit_bytes=VMEM_LIMIT),
        name="hidden_grad_" + half + ("" if by is not None else "_partial"),
    )(*args)


def weight_grad_kernel(tile, has_start, split, hidden, block, *refs):
    at = pl.ds(pl.multiple_of(pl.program_id(0) * tile, tile), tile)
    total = contract_first(hidden[...], block[...])
    if has_start:
        total = total + refs[0][at, :].astype(F32)
    total = total.astype(BF16)
    if not split:
        refs[-1][at, :] = total
        return
    send, keep = refs[-2:]
    half = send.shape[1]
    send[...] = total[:, :half]
    keep[...] = total[:, half:]


def weight_grad(block, hidden, start=None, split=True):
    (tok, ff), cols = hidden.shape, block.shape[1]
    tile = pick_tile(ff, 256)
    in_specs = [pl.BlockSpec((tok, tile), lambda i: (0, i)), VMEM_SPEC]
    args = [hidden, in_vmem(block)]
    if start is not None:
        in_specs.append(VMEM_SPEC)
        args.append(in_vmem(start))
    if split:
        out_specs = [pl.BlockSpec((tile, cols // 2), lambda i: (i, 0))] * 2
        out_shape = [pltpu.HBM((ff, cols // 2), BF16), pltpu.VMEM((ff, cols // 2), BF16)]
    else:
        out_specs, out_shape = VMEM_SPEC, pltpu.VMEM((ff, cols), BF16)
    return pl.pallas_call(
        functools.partial(weight_grad_kernel, tile, start is not None, split),
        grid=(ff // tile,),
        in_specs=in_specs,
        out_specs=out_specs,
        out_shape=out_shape,
        cost_estimate=SHORT,
        compiler_params=pltpu.CompilerParams(vmem_limit_bytes=VMEM_LIMIT),
        name="weight_grad",
    )(*args)


def add_kernel(scale, a_ref, b_ref, out_ref):
    out_ref[...] = ((a_ref[...].astype(F32) + b_ref[...].astype(F32)) * scale).astype(BF16)


def scaled_sum(keep, got, scale):
    rows, cols = keep.shape
    spec = pl.BlockSpec((pick_tile(rows, 896), cols), lambda i: (i, 0))
    return pl.pallas_call(
        functools.partial(add_kernel, scale),
        grid=(rows // spec.block_shape[0],),
        in_specs=[spec] * 2,
        out_specs=spec,
        out_shape=pltpu.HBM((rows, cols), BF16),
        cost_estimate=SHORT,
        compiler_params=pltpu.CompilerParams(vmem_limit_bytes=VMEM_LIMIT * 3 // 2),
        name="scaled_sum",
    )(keep, got)


def on_device(out_grad, gate_pre, up_pre, down_weight):
    grad, gate, up = out_grad[0], gate_pre[0], up_pre[0]
    tok, ff = gate.shape
    d = grad.shape[1]
    dp, nt = lax.axis_size("dp"), lax.axis_size("tensor")
    chips = dp // 2
    cols = d // chips
    chip, pair = lax.axis_index("dp") // 2, lax.axis_index("tensor") // 2
    scale = 1.0 / math.sqrt(tok * dp)

    def shift(value, s):
        return lax.ppermute(
            value, "dp", [(2 * c + k, 2 * ((c + s) % chips) + k) for c in range(chips) for k in range(2)]
        )

    def swap_cores(value):
        return lax.ppermute(value, "dp", [(k, k ^ 1) for k in range(dp)])

    def columns_of(which):
        return lax.dynamic_slice(grad, (0, which * cols), (grad.shape[0], cols))

    hidden = hidden_of(gate, up)
    if nt == 4 and chips == 2:
        both_ways = lambda *pairs: [q for a, b in pairs for q in ((a, b), (b, a))]
        swap_pair = lambda v: lax.ppermute(v, "tensor", both_ways((0, 1), (2, 3)))
        swap_middle = lambda v: lax.ppermute(v, "tensor", both_ways((1, 2)))
        to_ends = lambda v: lax.ppermute(v, "tensor", [(1, 0), (2, 3)])

        mine, rest = together(columns_of(chip), columns_of(1 - chip))
        far, a1 = shift(rest, 1), swap_pair(mine)
        both = stack([far, rest])
        a1, first, weight = together(a1, mark_of([far], 10**6), down_weight)

        hidden_in = shift(hidden, 1)
        a23 = swap_pair(both)
        pair1 = in_token_order("early", tok // 2, [mine, a1], wait_for=[first])
        b1 = swap_middle(pair1)
        *weights, mark = load_weight(weight, chips)
        a23, mark = together(a23, mark)

        pair3 = in_token_order("early", tok // 2, [far, a23], wait_for=[mark])
        b3 = swap_middle(pair3)
        pair2 = in_token_order("early", tok // 2, [rest, a23], swapped_from=tok // 4, cost=BRIEF)
        b1, mark = together(b1, mark_of([pair2], 1))

        c1 = to_ends(b1)
        outs = hidden_grad("early", [[pair1], [pair2]], weights, tok, None, (gate, up), wait_for=[mark])
        b3, c1, outs, pair2 = together(b3, c1, outs, pair2)

        shard = tok // 4
        c3, b2 = to_ends(b3), swap_middle(take_rows([pair2], 0, shard))
        partial = hidden_grad("late", [[b1, c1]], weights[:1], tok)
        hidden, partial = together(hidden, partial)
        block = in_token_order("all", tok, [pair1, b1, c1], by_core=True)
        own = weight_grad(block, hidden, split=False)
        first = mark_of([own], 1)
        b2, partial, first = together(b2, partial, first)

        c2 = to_ends(b2)
        c3, hidden_in, partial, first = together(c3, hidden_in, partial, first)
        rest2 = shift(take_rows([b3, c3], shard, shard), 1)
        block = in_token_order("all", tok, [pair3, b3, c3], by_core=True, wait_for=[first])
        send, keep = weight_grad(block, hidden_in, own)
        got = swap_cores(send)
        c2, rest2, send, partial = together(c2, rest2, send, partial)
        outs = hidden_grad("late", [[b2, c2, rest2]], weights[1:], tok, partial, (gate, up), outs, [send])
        got, outs = together(got, outs)
        down_grad = scaled_sum(keep, got, scale)
    else:
        gather = lambda v: lax.all_gather(v, "tensor", axis=0, tiled=True)
        hiddens = [hidden] + [shift(hidden, s) for s in range(1, chips)]

        def by_core(value):
            return jnp.where(lax.axis_index("dp") % 2 == 0, jnp.roll(value, cols // 2, axis=1), value)

        blocks = [by_core(gather(columns_of(chip)))]
        blocks += [by_core(gather(shift(columns_of((chip + s) % chips), s))) for s in range(1, chips)]
        total = None
        for block, part in zip(blocks[:-1], hiddens[:-1]):
            total = weight_grad(block, part, total, split=False)
        send, keep = weight_grad(blocks[-1], hiddens[-1], total)
        outs = hidden_grad("all", [[gather(grad)]], load_weight(down_weight, 1)[:1], tok, None, (gate, up))
        down_grad = scaled_sum(keep, swap_cores(send), scale)
    return (outs[0][None], outs[1][None], down_grad)


def solution(mesh):
    return jax.shard_map(
        on_device,
        mesh=mesh,
        in_specs=(
            P("dp", ("groups", "tensor"), None),
            P("dp", "groups", "tensor"),
            P("dp", "groups", "tensor"),
            P("tensor", None),
        ),
        out_specs=(
            P("dp", "groups", "tensor"),
            P("dp", "groups", "tensor"),
            P(("groups", "tensor"), "dp"),
        ),
        check_vma=False,
    )
```

```python
import functools
import math

import jax
import jax.numpy as jnp
from jax import lax
from jax.experimental import pallas as pl
from jax.experimental.pallas import tpu as pltpu
from jax.sharding import PartitionSpec as P

VMEM_LIMIT = 10 * 1024 * 1024
F32, BF16 = jnp.float32, jnp.bfloat16
SHORT = pl.CostEstimate(flops=1, bytes_accessed=1, transcendentals=0)
BRIEF = pl.CostEstimate(flops=1, bytes_accessed=10**6, transcendentals=0)
LONG = pl.CostEstimate(flops=10**12, bytes_accessed=10**9, transcendentals=0)
ANY_SPEC = pl.BlockSpec(memory_space=pl.ANY)
VMEM_SPEC = pl.BlockSpec(memory_space=pltpu.VMEM)


def pick_tile(extent, cap):
    return max(t for t in range(128, cap + 1, 128) if extent % t == 0)


def together(*values):
    return lax.optimization_barrier(values)


def sigmoid(x):
    return 0.5 + 0.5 * jnp.tanh(0.5 * x)


def contract_last(a, b):
    return lax.dot_general(a, b, (((1,), (1,)), ((), ())), preferred_element_type=F32)


def contract_first(a, b):
    return lax.dot_general(a, b, (((0,), (0,)), ((), ())), preferred_element_type=F32)


def in_vmem(value):
    return pltpu.with_memory_space_constraint(value, pltpu.VMEM)


def in_hbm(values):
    return [pltpu.with_memory_space_constraint(v, pltpu.HBM) for v in values]


def place_shards(parts, half, into, sem, start, by_core=False, swapped_from=0):
    act = (lambda c: c.start()) if start else (lambda c: c.wait())
    z = lax.axis_index("tensor")
    pair = z // 2
    parts = list(parts)
    slot = iter(range(16))

    def place(ref, row):
        rows = ref.shape[0]
        at = pl.ds(pl.multiple_of(row, 16), rows)
        if not by_core:
            act(pltpu.make_async_copy(ref, into.at[at], sem.at[next(slot)]))
            return
        cols = ref.shape[1] // 2
        for k in range(2):
            there = pl.multiple_of(jnp.where(lax.axis_index("dp") % 2 == k, 1, 0) * cols, cols)
            copy = pltpu.make_async_copy(
                ref.at[:, pl.ds(k * cols, cols)], into.at[at, pl.ds(there, cols)], sem.at[next(slot)]
            )
            act(copy)

    if half != "late":
        whole = parts[0].shape[0] * (2 if half == "early" else 4) == into.shape[0]
        base = 0 if half == "early" else pair * (into.shape[0] // 2)
        if whole:
            rows = parts[0].shape[0]
            place(parts.pop(0), base + (z % 2) * rows)
            place(parts.pop(0).at[pl.ds(swapped_from, rows)], base + (1 - z % 2) * rows)
        else:
            place(parts.pop(0), base)
    if half != "early":
        base = 0 if half == "late" else (1 - pair) * (into.shape[0] // 2)
        middle = jnp.logical_or(z == 1, z == 2)
        if len(parts) == 3:
            place(parts[2], base + parts[0].shape[0])

        @pl.when(middle)
        def _():
            place(parts[0], base)

        @pl.when(jnp.logical_not(middle))
        def _():
            place(parts[1], base)


def move_kernel(half, by_core, swapped_from, n_parts, *refs):
    parts, (into, sem) = refs[:n_parts], refs[-2:]
    for start in (True, False):
        place_shards(parts, half, into, sem, start, by_core, swapped_from)


def in_token_order(half, rows, parts, by_core=False, swapped_from=0, wait_for=(), cost=None):
    cols = parts[0].shape[1]
    return pl.pallas_call(
        functools.partial(move_kernel, half, by_core, swapped_from, len(parts)),
        in_specs=[ANY_SPEC] * (len(parts) + len(wait_for)),
        out_specs=VMEM_SPEC,
        out_shape=pltpu.VMEM((rows, cols), BF16),
        scratch_shapes=[pltpu.SemaphoreType.DMA((16,))],
        cost_estimate=cost,
        compiler_params=pltpu.CompilerParams(vmem_limit_bytes=VMEM_LIMIT),
        name="in_token_order",
    )(*parts, *in_hbm(wait_for))


def stack_kernel(*refs):
    parts, into, sem = refs[:-2], refs[-2], refs[-1]
    copies = []
    for k, part in enumerate(parts):
        rows = part.shape[0]
        copies.append(pltpu.make_async_copy(part, into.at[pl.ds(k * rows, rows)], sem.at[k]))
    for copy in copies:
        copy.start()
    for copy in copies:
        copy.wait()


def stack(parts):
    rows, cols = parts[0].shape
    return pl.pallas_call(
        stack_kernel,
        in_specs=[ANY_SPEC] * len(parts),
        out_specs=VMEM_SPEC,
        out_shape=pltpu.VMEM((rows * len(parts), cols), BF16),
        scratch_shapes=[pltpu.SemaphoreType.DMA((len(parts),))],
        compiler_params=pltpu.CompilerParams(vmem_limit_bytes=VMEM_LIMIT),
        name="stack",
    )(*parts)


def take_rows_kernel(row, *refs):
    parts, out, sem = refs[:-2], refs[-2], refs[-1]
    z = lax.axis_index("tensor")
    middle = jnp.logical_or(z == 1, z == 2)
    here = [None] if len(parts) == 1 else [middle, jnp.logical_not(middle)]

    def take(part):
        copy = pltpu.make_async_copy(part.at[pl.ds(row, out.shape[0])], out, sem)
        copy.start()
        copy.wait()

    for part, condition in zip(parts, here):
        if condition is None:
            take(part)
        else:
            pl.when(condition)(functools.partial(take, part))


def take_rows(parts, row, rows):
    return pl.pallas_call(
        functools.partial(take_rows_kernel, row),
        in_specs=[ANY_SPEC] * len(parts),
        out_specs=VMEM_SPEC,
        out_shape=pltpu.VMEM((rows, parts[0].shape[1]), BF16),
        scratch_shapes=[pltpu.SemaphoreType.DMA],
        compiler_params=pltpu.CompilerParams(vmem_limit_bytes=VMEM_LIMIT),
        name="take_rows",
    )(*parts)


def mark_kernel(*refs):
    out = refs[-1]
    out[...] = jnp.zeros(out.shape, out.dtype)


def mark_of(values, cost):
    return pl.pallas_call(
        mark_kernel,
        in_specs=[ANY_SPEC] * len(values),
        out_specs=pl.BlockSpec((8, 128), lambda: (0, 0)),
        out_shape=pltpu.HBM((8, 128), F32),
        cost_estimate=pl.CostEstimate(flops=1, bytes_accessed=cost, transcendentals=0),
        compiler_params=pltpu.CompilerParams(vmem_limit_bytes=VMEM_LIMIT),
        name="mark",
    )(*values)


def load_weight_kernel(weight, *refs):
    outs, mark, sem = refs[:-2], refs[-2], refs[-1]
    chip = lax.axis_index("dp") // 2
    copies = []
    for s, out in enumerate(outs):
        width = out.shape[1]
        at = pl.multiple_of(lax.rem(chip + s, len(outs)) * width, width)
        copies.append(pltpu.make_async_copy(weight.at[:, pl.ds(at, width)], out, sem.at[s]))
    for copy in copies:
        copy.start()
    mark[...] = jnp.zeros(mark.shape, mark.dtype)
    for copy in copies:
        copy.wait()


def load_weight(weight, blocks):
    ff, d = weight.shape
    return pl.pallas_call(
        load_weight_kernel,
        in_specs=[ANY_SPEC],
        out_specs=[VMEM_SPEC] * blocks + [pl.BlockSpec((8, 128), lambda: (0, 0))],
        out_shape=[pltpu.VMEM((ff, d // blocks), BF16)] * blocks + [pltpu.HBM((8, 128), F32)],
        scratch_shapes=[pltpu.SemaphoreType.DMA((blocks,))],
        cost_estimate=SHORT,
        compiler_params=pltpu.CompilerParams(vmem_limit_bytes=VMEM_LIMIT),
        name="load_weight",
    )(*in_hbm([weight]))


def hidden_kernel(gate_ref, up_ref, hidden_ref):
    gate, up = gate_ref[...].astype(F32), up_ref[...].astype(F32)
    hidden_ref[...] = (gate * sigmoid(gate) * up).astype(BF16)


def hidden_of(gate, up):
    tok, ff = gate.shape
    rows = next(r for r in (64, 32, 16) if tok % r == 0)
    spec = pl.BlockSpec((rows, ff), lambda i: (i, 0))
    return pl.pallas_call(
        hidden_kernel,
        grid=(tok // rows,),
        in_specs=[spec] * 2,
        out_specs=spec,
        out_shape=pltpu.HBM((tok, ff), BF16),
        cost_estimate=SHORT,
        compiler_params=pltpu.CompilerParams(vmem_limit_bytes=VMEM_LIMIT),
        name="hidden",
    )(*in_hbm([gate, up]))


def hidden_grad_kernel(half, counts, tile, has_partial, finish, *refs):
    refs = list(refs)
    streams = [[refs.pop(0) for _ in range(count)] for count in counts]
    weights = [refs.pop(0) for _ in counts]
    partial = refs.pop(0) if has_partial else None
    if sum(counts) == len(counts):
        lhs = [stream[0] for stream in streams]
    else:
        sem = refs.pop()
        lhs = refs[-len(counts) :]
        refs = refs[: -len(counts)]

        @pl.when(pl.program_id(0) == 0)
        def _():
            for start in (True, False):
                for s, parts in enumerate(streams):
                    place_shards(parts, half, lhs[s], sem.at[s], start)

    step = pl.program_id(0)
    at = pl.multiple_of(step * tile, tile)
    total = partial[...] if has_partial else None
    for left, weight in zip(lhs, weights):
        term = contract_last(left[...], weight[pl.ds(at, tile), :])
        total = term if total is None else total + term
    if not finish:
        refs[-1][...] = total
        return
    gate, up = refs[0][...].astype(F32), refs[1][...].astype(F32)
    gate_out, up_out = refs[-2:]
    sig = sigmoid(gate)
    gate_out[...] = (total * up * sig * (1.0 + gate * (1.0 - sig))).astype(BF16)
    up_out[...] = (total * (gate * sig)).astype(BF16)


def hidden_grad(half, streams, weights, tok, partial=None, by=None, outs=None, wait_for=()):
    ff = weights[0].shape[0]
    rows = tok if half == "all" else tok // 2
    tile = pick_tile(ff, 512 if half == "early" else 896)

    def place(i):
        pair = lax.axis_index("tensor") // 2
        return ({"all": 0, "early": pair, "late": 1 - pair}[half], i)

    block = pl.BlockSpec((rows, tile), place)
    part_block = pl.BlockSpec((rows, tile), lambda i: (0, i))
    if all(len(s) == 1 for s in streams):
        in_specs, args, scratch = [VMEM_SPEC] * len(streams), [in_vmem(s[0]) for s in streams], []
    else:
        args = [part for s in streams for part in s]
        in_specs = [ANY_SPEC] * len(args)
        scratch = [pltpu.VMEM((rows, w.shape[1]), BF16) for w in weights] + [
            pltpu.SemaphoreType.DMA((len(weights), 16))
        ]
    in_specs += [VMEM_SPEC] * len(weights)
    args += [in_vmem(w) for w in weights]
    aliases = {}
    if partial is not None:
        in_specs.append(part_block)
        args += in_hbm([partial])
    if by is not None:
        in_specs += [block] * 2
        args += in_hbm(by)
    in_specs += [ANY_SPEC] * len(wait_for)
    args += in_hbm(wait_for)
    if by is not None:
        out_shape, out_specs = [pltpu.HBM((tok, ff), BF16)] * 2, [block] * 2
        if outs is not None:
            aliases = {len(args): 0, len(args) + 1: 1}
            in_specs += [ANY_SPEC] * 2
            args += in_hbm(outs)
    else:
        out_shape, out_specs = pltpu.HBM((rows, ff), F32), part_block
    return pl.pallas_call(
        functools.partial(
            hidden_grad_kernel,
            half,
            tuple(len(s) for s in streams),
            tile,
            partial is not None,
            by is not None,
        ),
        grid=(ff // tile,),
        in_specs=in_specs,
        out_specs=out_specs,
        scratch_shapes=scratch,
        out_shape=out_shape,
        input_output_aliases=aliases,
        cost_estimate=LONG if outs is not None else SHORT,
        compiler_params=pltpu.CompilerParams(vmem_limit_bytes=VMEM_LIMIT * (3 if outs is not None else 2) // 2),
        name="hidden_grad_" + half + ("" if by is not None else "_partial"),
    )(*args)


def weight_grad_kernel(tile, has_start, split, hidden, block, *refs):
    at = pl.ds(pl.multiple_of(pl.program_id(0) * tile, tile), tile)
    total = contract_first(hidden[...], block[...])
    if has_start:
        total = total + refs[0][at, :].astype(F32)
    total = total.astype(BF16)
    if not split:
        refs[-1][at, :] = total
        return
    send, keep = refs[-2:]
    half = send.shape[1]
    send[...] = total[:, :half]
    keep[...] = total[:, half:]


def weight_grad(block, hidden, start=None, split=True):
    (tok, ff), cols = hidden.shape, block.shape[1]
    tile = pick_tile(ff, 256)
    in_specs = [pl.BlockSpec((tok, tile), lambda i: (0, i)), VMEM_SPEC]
    args = [hidden, in_vmem(block)]
    if start is not None:
        in_specs.append(VMEM_SPEC)
        args.append(in_vmem(start))
    if split:
        out_specs = [pl.BlockSpec((tile, cols // 2), lambda i: (i, 0))] * 2
        out_shape = [pltpu.HBM((ff, cols // 2), BF16), pltpu.VMEM((ff, cols // 2), BF16)]
    else:
        out_specs, out_shape = VMEM_SPEC, pltpu.VMEM((ff, cols), BF16)
    return pl.pallas_call(
        functools.partial(weight_grad_kernel, tile, start is not None, split),
        grid=(ff // tile,),
        in_specs=in_specs,
        out_specs=out_specs,
        out_shape=out_shape,
        cost_estimate=SHORT,
        compiler_params=pltpu.CompilerParams(vmem_limit_bytes=VMEM_LIMIT),
        name="weight_grad",
    )(*args)


def add_kernel(scale, a_ref, b_ref, out_ref):
    out_ref[...] = ((a_ref[...].astype(F32) + b_ref[...].astype(F32)) * scale).astype(BF16)


def scaled_sum(keep, got, scale):
    rows, cols = keep.shape
    spec = pl.BlockSpec((pick_tile(rows, 896), cols), lambda i: (i, 0))
    return pl.pallas_call(
        functools.partial(add_kernel, scale),
        grid=(rows // spec.block_shape[0],),
        in_specs=[spec] * 2,
        out_specs=spec,
        out_shape=pltpu.HBM((rows, cols), BF16),
        cost_estimate=SHORT,
        compiler_params=pltpu.CompilerParams(vmem_limit_bytes=VMEM_LIMIT * 3 // 2),
        name="scaled_sum",
    )(keep, got)


def on_device(out_grad, gate_pre, up_pre, down_weight):
    grad, gate, up = out_grad[0], gate_pre[0], up_pre[0]
    tok, ff = gate.shape
    d = grad.shape[1]
    dp, nt = lax.axis_size("dp"), lax.axis_size("tensor")
    chips = dp // 2
    cols = d // chips
    chip, pair = lax.axis_index("dp") // 2, lax.axis_index("tensor") // 2
    scale = 1.0 / math.sqrt(tok * dp)

    def shift(value, s):
        return lax.ppermute(
            value, "dp", [(2 * c + k, 2 * ((c + s) % chips) + k) for c in range(chips) for k in range(2)]
        )

    def swap_cores(value):
        return lax.ppermute(value, "dp", [(k, k ^ 1) for k in range(dp)])

    def columns_of(which):
        return lax.dynamic_slice(grad, (0, which * cols), (grad.shape[0], cols))

    hidden = hidden_of(gate, up)
    if nt == 4 and chips == 2:
        both_ways = lambda *pairs: [q for a, b in pairs for q in ((a, b), (b, a))]
        swap_pair = lambda v: lax.ppermute(v, "tensor", both_ways((0, 1), (2, 3)))
        swap_middle = lambda v: lax.ppermute(v, "tensor", both_ways((1, 2)))
        to_ends = lambda v: lax.ppermute(v, "tensor", [(1, 0), (2, 3)])

        mine, rest = together(columns_of(chip), columns_of(1 - chip))
        far, a1 = shift(rest, 1), swap_pair(mine)
        both = stack([far, rest])
        a1, first, weight = together(a1, mark_of([far], 10**6), down_weight)

        hidden_in = shift(hidden, 1)
        a23 = swap_pair(both)
        pair1 = in_token_order("early", tok // 2, [mine, a1], wait_for=[first])
        b1 = swap_middle(pair1)
        *weights, mark = load_weight(weight, chips)
        a23, mark = together(a23, mark)

        pair3 = in_token_order("early", tok // 2, [far, a23], wait_for=[mark])
        b3 = swap_middle(pair3)
        pair2 = in_token_order("early", tok // 2, [rest, a23], swapped_from=tok // 4, cost=BRIEF)
        b1, mark = together(b1, mark_of([pair2], 1))

        c1 = to_ends(b1)
        outs = hidden_grad("early", [[pair1], [pair2]], weights, tok, None, (gate, up), wait_for=[mark])
        b3, c1, outs, pair2 = together(b3, c1, outs, pair2)

        shard = tok // 4
        c3, b2 = to_ends(b3), swap_middle(take_rows([pair2], 0, shard))
        partial = hidden_grad("late", [[b1, c1]], weights[:1], tok)
        hidden, partial = together(hidden, partial)
        block = in_token_order("all", tok, [pair1, b1, c1], by_core=True)
        own = weight_grad(block, hidden, split=False)
        first = mark_of([own], 1)
        b2, partial, first = together(b2, partial, first)

        c2 = to_ends(b2)
        c3, hidden_in, partial, first = together(c3, hidden_in, partial, first)
        rest2 = shift(take_rows([b3, c3], shard, shard), 1)
        block = in_token_order("all", tok, [pair3, b3, c3], by_core=True, wait_for=[first])
        send, keep = weight_grad(block, hidden_in, own)
        got = swap_cores(send)
        c2, rest2, send, partial = together(c2, rest2, send, partial)
        outs = hidden_grad("late", [[b2, c2, rest2]], weights[1:], tok, partial, (gate, up), outs, [send])
        got, outs = together(got, outs)
        down_grad = scaled_sum(keep, got, scale)
    else:
        gather = lambda v: lax.all_gather(v, "tensor", axis=0, tiled=True)
        hiddens = [hidden] + [shift(hidden, s) for s in range(1, chips)]

        def by_core(value):
            return jnp.where(lax.axis_index("dp") % 2 == 0, jnp.roll(value, cols // 2, axis=1), value)

        blocks = [by_core(gather(columns_of(chip)))]
        blocks += [by_core(gather(shift(columns_of((chip + s) % chips), s))) for s in range(1, chips)]
        total = None
        for block, part in zip(blocks[:-1], hiddens[:-1]):
            total = weight_grad(block, part, total, split=False)
        send, keep = weight_grad(blocks[-1], hiddens[-1], total)
        outs = hidden_grad("all", [[gather(grad)]], load_weight(down_weight, 1)[:1], tok, None, (gate, up))
        down_grad = scaled_sum(keep, swap_cores(send), scale)
    return (outs[0][None], outs[1][None], down_grad)


def solution(mesh):
    return jax.shard_map(
        on_device,
        mesh=mesh,
        in_specs=(
            P("dp", ("groups", "tensor"), None),
            P("dp", "groups", "tensor"),
            P("dp", "groups", "tensor"),
            P("tensor", None),
        ),
        out_specs=(
            P("dp", "groups", "tensor"),
            P("dp", "groups", "tensor"),
            P(("groups", "tensor"), "dp"),
        ),
        check_vma=False,
    )
```
